32 devices in a mesh: vox: 8 (over z, x), chan: 4 (over y, core).
Axes of the slice: x: 2, y: 2, z: 4, core: 2. Of those that a mesh axis runs over, the one named last changes fastest.
Arguments:
- model_blocks: bfloat16 [2944, 128, 128], P(('vox', 'chan')), may hold values from -0.15625 to 0.15625
- start_image: float32 [256, 32, 128], P('vox'), may hold values from 0 to 2
- measured: float32 [256, 32, 128], P(('vox', 'chan')), may hold values from -6 to 6
- step_size: float32 [32], replicated, may hold values from 0.05 to 0.25
- sent_tiles: int32 [8, 8, 4], P('vox'), may hold values from -1 to 31, as said below
- block_rows: int32 [2944], P(('vox', 'chan')), may hold values from 0 to 7
- block_slots: int32 [2944], P(('vox', 'chan')), may hold values from 0 to 31, as said below
Outputs:
- estimate: float32 [256, 32, 128], P('vox')
- residual: float32 [256, 32, 128], P(('vox', 'chan'))
The draws below stay inside these ranges and needn't reach their ends.
Inputs may be any that keep to these rules, and one draw needn't show every extreme that they name: `sent_tiles`: an entry is -1 for an unused slot, else a tile of slab j; the used slots of one pair (j, v) come first, hold distinct tiles, number 1 to 4, and slab v always uses all 4 slots for itself. `block_slots`: every block names a used slot of its own device's vox index v, that is sent_tiles[j, v, s] is not -1.
All inputs are finite; a program needn't handle non-finite values.
Results may differ from the reference program's by a relative error of at most 0.0045.
Values may be sent and summed in bfloat16 or wider, within the bound.
No kernel may reach another device: no remote copies, remote signals or barrier semaphores. Data moves between devices by JAX's collectives and lax.ppermute only.
A program may use at most 64 MiB of HBM per device.

```python
import math
import jax
import jax.numpy as jnp
from jax import lax

BLOCK_SIZE = 128
WAVELENGTHS = 32
TILES_DEV = 32
ROWS_DEV = 8
BLOCKS_DEV = 92
SLOT_CAP = 4
ITERATIONS = 4
ALL_TILES = 256
ALL_ROWS = 256
ALL_BLOCKS = 2944
N_VOX = 8
N_CHAN = 4


def slot_counts(key):
    inner_key = jax.random.fold_in(key, 7)
    first_key, second_key = jax.random.split(inner_key)
    height = jax.random.randint(first_key, (N_VOX, N_VOX), 0, SLOT_CAP)
    switch = jax.random.randint(second_key, (N_VOX, N_VOX), 0, 2)
    counts = 1 + height * switch
    diagonal = jnp.eye(N_VOX, dtype=jnp.int32)
    return (counts * (1 - diagonal) + SLOT_CAP * diagonal).astype(jnp.int32)


def draw_sent_tiles(key, part):
    counts = slot_counts(key)
    scores = jax.random.randint(jax.random.fold_in(key, 8), (N_VOX, N_VOX, TILES_DEV), 0, 1 << 20)
    scores = scores * TILES_DEV + jnp.arange(TILES_DEV, dtype=jnp.int32)
    ranking = jnp.argsort(scores, axis=-1, stable=True)[:, :, :SLOT_CAP].astype(jnp.int32)
    slot_range = jnp.arange(SLOT_CAP, dtype=jnp.int32)[None, None, :]
    return jnp.where(slot_range < counts[:, :, None], ranking, -1).astype(jnp.int32)


def draw_block_slots(key, part):
    counts = slot_counts(key)
    used_slots = (jnp.arange(SLOT_CAP, dtype=jnp.int32)[None, None, :] < counts[:, :, None]).astype(jnp.int32)
    by_target = jnp.transpose(used_slots, (1, 0, 2)).reshape(N_VOX, N_VOX * SLOT_CAP)
    running = jnp.cumsum(by_target, axis=1)
    totals = running[:, -1]
    per_vox = N_CHAN * BLOCKS_DEV
    limits = jnp.repeat(totals, per_vox).reshape(N_VOX, per_vox)
    picked_rank = jax.random.randint(jax.random.fold_in(key, 9), (N_VOX, per_vox), 0, limits)
    found = jax.vmap(lambda cumulative, wanted: jnp.searchsorted(cumulative, wanted, side='right'))(running, picked_rank)
    return found.reshape(N_VOX * per_vox).astype(jnp.int32)


def plant(entries, key, low, high):
    spot = [jax.random.randint(jax.random.fold_in(key, axis), (), 0, length) for axis, length in enumerate(entries.shape)]
    longest = entries.shape.index(max(entries.shape))
    neighbour = spot[:longest] + [(spot[longest] + 1) % entries.shape[longest]] + spot[longest + 1:]
    return entries.at[tuple(spot)].set(low).at[tuple(neighbour)].set(high)


def shard_levels(stream_key, extent, cuts, least, high):
    def one(position, shards_of):
        draws = jax.random.uniform(jax.random.fold_in(jax.random.fold_in(stream_key, 6), position), (shards_of,), jnp.float32, least / len(cuts), high / len(cuts))
        return jnp.repeat(jnp.exp(draws), extent[position] // shards_of).reshape((-1,) + (1,) * (len(extent) - position - 1))

    factor_of = one(*cuts[0])
    for cut in cuts[1:]:
        factor_of = factor_of * one(*cut)
    return factor_of


def noise(own_key, extent, spread, limit, shards=(), held_as=jnp.bfloat16):
    array = jax.random.normal(own_key, extent, jnp.float32) * spread
    if len(shards) > 0:
        array = shard_levels(own_key, extent, shards, -0.22, 0.18) * array
    return jnp.clip(array, min=-limit, max=limit).astype(held_as)


def setup_inputs(seed: int = 0) -> dict:
    splits = jax.random.split(jax.random.key(seed), 8)
    return {
        "model_blocks": noise(splits[0], (ALL_BLOCKS, BLOCK_SIZE, BLOCK_SIZE), (BLOCKS_DEV // ROWS_DEV * BLOCK_SIZE) ** -0.5, 0.15625, ((0, 32),)),
        "start_image": jnp.clip(2.0 * jax.random.uniform(splits[1], (ALL_TILES, WAVELENGTHS, BLOCK_SIZE), jnp.float32) ** shard_levels(splits[1], (ALL_TILES, WAVELENGTHS, BLOCK_SIZE), ((0, 8),), -0.2, 0.2), 0.0, 2.0),
        "measured": noise(splits[2], (ALL_ROWS, WAVELENGTHS, BLOCK_SIZE), 1.0, 6.0, ((0, 32),), jnp.float32),
        "step_size": jnp.clip(jnp.exp(jax.random.uniform(splits[3], (WAVELENGTHS,), jnp.float32, math.log(0.05), math.log(0.25))), 0.05, 0.25),
        "sent_tiles": draw_sent_tiles(jax.random.fold_in(splits[7], 71), 0),
        "block_rows": plant(jax.random.randint(splits[5], (ALL_BLOCKS,), 0, ROWS_DEV), jax.random.fold_in(splits[5], 1), 0, ROWS_DEV - 1).astype(jnp.int32),
        "block_slots": draw_block_slots(jax.random.fold_in(splits[7], 71), 0),
    }


def reference(model_blocks, start_image, measured, step_size, sent_tiles, block_rows, block_slots):
    devices = N_VOX * N_CHAN
    owner_dev = (jnp.arange(ALL_BLOCKS) // BLOCKS_DEV).astype(jnp.int32)
    holder_vox = (owner_dev // N_CHAN).astype(jnp.int32)
    source = (block_slots // SLOT_CAP).astype(jnp.int32)
    within = (block_slots % SLOT_CAP).astype(jnp.int32)
    tile_index = (source * TILES_DEV + sent_tiles[source, holder_vox, within]).astype(jnp.int32)
    blocks = model_blocks.reshape(devices, BLOCKS_DEV, BLOCK_SIZE, BLOCK_SIZE)
    tiles_by = tile_index.reshape(devices, BLOCKS_DEV)
    rows_by = block_rows.astype(jnp.int32).reshape(devices, BLOCKS_DEV)
    step_gains = step_size[None, :, None]
    estimate = start_image
    residual = measured
    for iteration in range(ITERATIONS):
        rounded = estimate.astype(jnp.bfloat16)

        def forward_one(inputs):
            blocks_here, tiles_here, rows_here = inputs
            picked = rounded[tiles_here].astype(jnp.float32)
            products = jnp.einsum("bwv,bsv->bws", picked, blocks_here.astype(jnp.float32), precision=lax.Precision.HIGHEST)
            return jax.ops.segment_sum(products, rows_here, num_segments=ROWS_DEV)

        predicted = lax.map(forward_one, (blocks, tiles_by, rows_by)).reshape(ALL_ROWS, WAVELENGTHS, BLOCK_SIZE)
        residual = measured - predicted
        narrow = residual.astype(jnp.bfloat16).reshape(devices, ROWS_DEV, WAVELENGTHS, BLOCK_SIZE)

        def adjoint_one(running_sum, inputs):
            blocks_here, tiles_here, rows_here, residual_here = inputs
            picked = residual_here[rows_here].astype(jnp.float32)
            adjoint_terms = jnp.einsum("bws,bsv->bwv", picked, blocks_here.astype(jnp.float32), precision=lax.Precision.HIGHEST)
            return running_sum.at[tiles_here].add(adjoint_terms), None

        gradient = lax.scan(adjoint_one, jnp.zeros(start_image.shape, jnp.float32), (blocks, tiles_by, rows_by, narrow))[0]
        estimate = jnp.maximum(estimate + step_gains * gradient, 0.0)
    return estimate, residual
```

```python
import functools
import math

import jax
import jax.numpy as jnp
from jax import lax
from jax.experimental import pallas as pl
from jax.experimental.pallas import tpu as pltpu
from jax.sharding import PartitionSpec as P

ITERATIONS = 4
LOW = 8


VMEM = pl.BlockSpec(memory_space=pltpu.VMEM)
SMEM = pl.BlockSpec(memory_space=pltpu.SMEM)
PARAMS = pltpu.CompilerParams(vmem_limit_bytes=32 * 1024 * 1024)


def model_kernel(vox_count, chan_count, per, low, slots, rows, model, measured, *refs):
    arrived = refs[:low]
    own, *sent = refs[low : low + chan_count]
    residual, tiles, narrow, sums = refs[low + chan_count :]
    wide = vox_count * per
    for e in range(vox_count):
        for d in range(chan_count):
            place = d * wide + e * per
            tiles[place : place + per] = arrived[e % low][e // low, d * per : (d + 1) * per]
    residual[...] = measured[...]
    sums[...] = jnp.zeros_like(sums)
    count = model.shape[0]
    for k in range(count):
        part = lax.dot_general(
            tiles[slots[k]],
            model[k],
            (((1,), (1,)), ((), ())),
            preferred_element_type=jnp.float32,
        )
        residual[rows[k]] -= part
    narrow[...] = residual[...].astype(jnp.bfloat16)
    for k in range(count):
        part = jnp.dot(narrow[rows[k]], model[k], preferred_element_type=jnp.float32)
        sums[slots[k]] += part
    own[...] = sums[:wide]
    for d, out in enumerate(sent, 1):
        out[...] = sums[d * wide : (d + 1) * wide].astype(jnp.bfloat16)


def reduce_kernel(vox_count, chan_count, per, low, own, *refs):
    received, outs = refs[: chan_count - 1], refs[chan_count - 1 :]
    total = own[...]
    for piece in received:
        total = total + piece[...].astype(jnp.float32)
    total = total.astype(jnp.bfloat16)
    for e in range(vox_count):
        outs[e % low][e // low] = total[e * per : (e + 1) * per]


def place_of(ids, table, per, d, e, p):
    return jnp.maximum(table[ids[0] ^ e, (ids[1] ^ d) * per + p], 0)


def pick_kernel(vox_count, chan_count, per, low, ids, table, image, *outs):
    for e in range(vox_count):
        for d in range(chan_count):
            for p in range(per):
                tile = place_of(ids, table, per, d, e, p)
                outs[e % low][e // low, d * per + p] = image[tile].astype(jnp.bfloat16)


def update_kernel(vox_count, chan_count, per, low, ids, table, gains, image, *refs):
    received = refs[:chan_count]
    estimate, *outs = refs[chan_count:-1]
    gradient = refs[-1]
    gradient[...] = jnp.zeros_like(gradient)
    for d in range(chan_count):
        for e in range(vox_count):
            for p in range(per):
                tile = place_of(ids, table, per, d, e, p)
                gradient[tile] += received[d][e * per + p].astype(jnp.float32)
    estimate[...] = jnp.maximum(image[...] + gains[...][None] * gradient[...], 0.0)
    if outs:
        pick_kernel(vox_count, chan_count, per, low, ids, table, estimate, *outs)


def shards(model_blocks, start_image, measured, step_size, sent_tiles, block_rows, block_slots):
    vox_count = lax.axis_size("vox")
    chan_count = lax.axis_size("chan")
    vox, chan = lax.axis_index("vox"), lax.axis_index("chan")
    table = sent_tiles[0]
    capacity = table.shape[1]
    per = capacity // chan_count
    tile_count, wave_count, width = start_image.shape
    row_count = measured.shape[0]
    slot_count = vox_count * capacity
    wide = vox_count * per
    low = math.gcd(vox_count, LOW)
    high = vox_count // low
    tile = (wave_count, width)
    ids = jnp.stack([vox, chan]).astype(jnp.int32)
    slab, slot = block_slots // capacity, block_slots % capacity
    places = (((slot // per) ^ chan) * vox_count + (slab ^ vox)) * per + slot % per
    gains = jnp.broadcast_to(step_size[:, None], tile)

    def shape(count, dtype):
        return jax.ShapeDtypeStruct((count, *tile), dtype)

    def group(count):
        return [jax.ShapeDtypeStruct((high, count, *tile), jnp.bfloat16)] * low

    def swap(array, axis, size, step):
        if step == 0:
            return array
        return lax.ppermute(array, axis, [(i, i ^ step) for i in range(size)])

    def exchange(pieces):
        pieces = [swap(piece, "vox", vox_count, e) for e, piece in enumerate(pieces)]
        if high == 1:
            return pieces
        both = jnp.stack(pieces)
        both = [swap(both[:, e], "vox", vox_count, e * low) for e in range(high)]
        return list(jnp.stack(both, axis=1))

    apply_model = pl.pallas_call(
        functools.partial(model_kernel, vox_count, chan_count, per, low),
        out_shape=(
            shape(wide, jnp.float32),
            *[shape(wide, jnp.bfloat16)] * (chan_count - 1),
            shape(row_count, jnp.float32),
        ),
        in_specs=[SMEM, SMEM, VMEM, VMEM] + [VMEM] * low,
        out_specs=[VMEM] * (chan_count + 1),
        scratch_shapes=[
            pltpu.VMEM((slot_count, *tile), jnp.bfloat16),
            pltpu.VMEM((row_count, *tile), jnp.bfloat16),
            pltpu.VMEM((slot_count, *tile), jnp.float32),
        ],
        compiler_params=PARAMS,
        name="model",
    )
    reduce_parts = pl.pallas_call(
        functools.partial(reduce_kernel, vox_count, chan_count, per, low),
        out_shape=group(per),
        in_specs=[VMEM] * chan_count,
        out_specs=[VMEM] * low,
        compiler_params=PARAMS,
        name="reduce",
    )
    pick = pl.pallas_call(
        functools.partial(pick_kernel, vox_count, chan_count, per, low),
        out_shape=group(capacity),
        in_specs=[SMEM, SMEM, VMEM],
        out_specs=[VMEM] * low,
        compiler_params=PARAMS,
        name="pick",
    )

    def update(last):
        outs = [] if last else group(capacity)
        return pl.pallas_call(
            functools.partial(update_kernel, vox_count, chan_count, per, low),
            out_shape=[shape(tile_count, jnp.float32)] + outs,
            in_specs=[SMEM, SMEM, VMEM, VMEM] + [VMEM] * chan_count,
            out_specs=[VMEM] * (len(outs) + 1),
            scratch_shapes=[pltpu.VMEM((tile_count, *tile), jnp.float32)],
            compiler_params=PARAMS,
            name="update",
        )

    estimate = start_image
    outgoing = pick(ids, table, start_image)
    for iteration in range(ITERATIONS):
        own, *rest = apply_model(
            places, block_rows, model_blocks, measured, *exchange(outgoing)
        )
        *partial, residual = rest
        received = [swap(piece, "chan", chan_count, d) for d, piece in enumerate(partial, 1)]
        totals = reduce_parts(own, *received)
        returned = jnp.stack(exchange(totals), axis=1).reshape(wide, *tile)
        spread = [swap(returned, "chan", chan_count, d) for d in range(chan_count)]
        estimate, *outgoing = update(iteration == ITERATIONS - 1)(
            ids, table, gains, estimate, *spread
        )
    return (estimate, residual)


def solution(mesh):
    in_specs = (
        P(("vox", "chan"), None, None),
        P("vox", None, None),
        P(("vox", "chan"), None, None),
        P(),
        P("vox", None, None),
        P(("vox", "chan")),
        P(("vox", "chan")),
    )
    out_specs = (P("vox", None, None), P(("vox", "chan"), None, None))
    return jax.shard_map(shards, mesh=mesh, in_specs=in_specs, out_specs=out_specs, check_vma=False)
```

```python
import functools

import jax
import jax.numpy as jnp
from jax import lax
from jax.experimental import pallas as pl
from jax.experimental.pallas import tpu as pltpu
from jax.sharding import PartitionSpec as P

ITERATIONS = 4


VMEM = pl.BlockSpec(memory_space=pltpu.VMEM)
SMEM = pl.BlockSpec(memory_space=pltpu.SMEM)
PARAMS = pltpu.CompilerParams(vmem_limit_bytes=32 * 1024 * 1024)


def stages_of(count):
    stages, radix, stride = [], 2, 1
    while stride < count:
        radix = min(radix, count // stride)
        stages.insert(0, (radix, stride))
        stride, radix = stride * radix, radix * 2
    rest = stages[0][1]
    where = {e: divmod(e, rest) for e in range(count)}
    moves, arrays = [], stages[0][0]
    for radix, stride in stages[1:]:
        for digit in range(1, radix):
            chosen = [e for e in range(count) if e // stride % radix == digit]
            moves.append((digit * stride, [where[e] for e in chosen]))
            where.update({e: (arrays, i) for i, e in enumerate(chosen)})
            arrays += 1
    return stages[0], moves, where


def model_kernel(where, chan_count, per, slots, rows, model, measured, *refs):
    pieces = 1 + max(array for array, _ in where.values())
    arrived = refs[:pieces]
    own, *sent = refs[pieces : pieces + chan_count]
    residual, tiles, narrow, sums = refs[pieces + chan_count :]
    wide = len(where) * per
    for e, (array, i) in where.items():
        for d in range(chan_count):
            place = d * wide + e * per
            tiles[place : place + per] = arrived[array][i, d * per : (d + 1) * per]
    residual[...] = measured[...]
    sums[...] = jnp.zeros_like(sums)
    count = model.shape[0]
    for k in range(count):
        part = lax.dot_general(
            tiles[slots[k]],
            model[k],
            (((1,), (1,)), ((), ())),
            preferred_element_type=jnp.float32,
        )
        residual[rows[k]] -= part
    narrow[...] = residual[...].astype(jnp.bfloat16)
    for k in range(count):
        part = jnp.dot(narrow[rows[k]], model[k], preferred_element_type=jnp.float32)
        sums[slots[k]] += part
    own[...] = sums[:wide]
    for d, out in enumerate(sent, 1):
        out[...] = sums[d * wide : (d + 1) * wide].astype(jnp.bfloat16)


def reduce_kernel(vox_count, chan_count, per, rest, own, *refs):
    received, outs = refs[: chan_count - 1], refs[chan_count - 1 :]
    total = own[...]
    for piece in received:
        total = total + piece[...].astype(jnp.float32)
    total = total.astype(jnp.bfloat16)
    for e in range(vox_count):
        outs[e // rest][e % rest] = total[e * per : (e + 1) * per]


def place_of(ids, table, per, d, e, p):
    return jnp.maximum(table[ids[0] ^ e, (ids[1] ^ d) * per + p], 0)


def pick_kernel(vox_count, chan_count, per, rest, ids, table, image, *outs):
    for e in range(vox_count):
        for d in range(chan_count):
            for p in range(per):
                tile = place_of(ids, table, per, d, e, p)
                outs[e // rest][e % rest, d * per + p] = image[tile].astype(jnp.bfloat16)


def update_kernel(vox_count, chan_count, per, rest, ids, table, gains, image, *refs):
    received = refs[:chan_count]
    estimate, *outs = refs[chan_count:-1]
    gradient = refs[-1]
    gradient[...] = jnp.zeros_like(gradient)
    for d in range(chan_count):
        for e in range(vox_count):
            for p in range(per):
                tile = place_of(ids, table, per, d, e, p)
                gradient[tile] += received[d][e * per + p].astype(jnp.float32)
    estimate[...] = jnp.maximum(image[...] + gains[...][None] * gradient[...], 0.0)
    if outs:
        pick_kernel(vox_count, chan_count, per, rest, ids, table, estimate, *outs)


def shards(model_blocks, start_image, measured, step_size, sent_tiles, block_rows, block_slots):
    vox_count = lax.axis_size("vox")
    chan_count = lax.axis_size("chan")
    vox, chan = lax.axis_index("vox"), lax.axis_index("chan")
    table = sent_tiles[0]
    capacity = table.shape[1]
    per = capacity // chan_count
    tile_count, wave_count, width = start_image.shape
    row_count = measured.shape[0]
    slot_count = vox_count * capacity
    wide = vox_count * per
    (first, rest), moves, where = stages_of(vox_count)
    tile = (wave_count, width)
    ids = jnp.stack([vox, chan]).astype(jnp.int32)
    slab, slot = block_slots // capacity, block_slots % capacity
    places = (((slot // per) ^ chan) * vox_count + (slab ^ vox)) * per + slot % per
    gains = jnp.broadcast_to(step_size[:, None], tile)

    def shape(count, dtype):
        return jax.ShapeDtypeStruct((count, *tile), dtype)

    def group(count):
        return [jax.ShapeDtypeStruct((rest, count, *tile), jnp.bfloat16)] * first

    def swap(array, axis, size, step):
        if step == 0:
            return array
        return lax.ppermute(array, axis, [(i, i ^ step) for i in range(size)])

    def exchange(pieces):
        pieces = [swap(piece, "vox", vox_count, h * rest) for h, piece in enumerate(pieces)]
        for step, chosen in moves:
            moved = jnp.stack([pieces[array][i] for array, i in chosen])
            pieces.append(swap(moved, "vox", vox_count, step))
        return pieces

    apply_model = pl.pallas_call(
        functools.partial(model_kernel, where, chan_count, per),
        out_shape=(
            shape(wide, jnp.float32),
            *[shape(wide, jnp.bfloat16)] * (chan_count - 1),
            shape(row_count, jnp.float32),
        ),
        in_specs=[SMEM, SMEM, VMEM, VMEM] + [VMEM] * (first + len(moves)),
        out_specs=[VMEM] * (chan_count + 1),
        scratch_shapes=[
            pltpu.VMEM((slot_count, *tile), jnp.bfloat16),
            pltpu.VMEM((row_count, *tile), jnp.bfloat16),
            pltpu.VMEM((slot_count, *tile), jnp.float32),
        ],
        compiler_params=PARAMS,
        name="model",
    )
    reduce_parts = pl.pallas_call(
        functools.partial(reduce_kernel, vox_count, chan_count, per, rest),
        out_shape=group(per),
        in_specs=[VMEM] * chan_count,
        out_specs=[VMEM] * first,
        compiler_params=PARAMS,
        name="reduce",
    )
    pick = pl.pallas_call(
        functools.partial(pick_kernel, vox_count, chan_count, per, rest),
        out_shape=group(capacity),
        in_specs=[SMEM, SMEM, VMEM],
        out_specs=[VMEM] * first,
        compiler_params=PARAMS,
        name="pick",
    )

    def update(last):
        outs = [] if last else group(capacity)
        return pl.pallas_call(
            functools.partial(update_kernel, vox_count, chan_count, per, rest),
            out_shape=[shape(tile_count, jnp.float32)] + outs,
            in_specs=[SMEM, SMEM, VMEM, VMEM] + [VMEM] * chan_count,
            out_specs=[VMEM] * (len(outs) + 1),
            scratch_shapes=[pltpu.VMEM((tile_count, *tile), jnp.float32)],
            compiler_params=PARAMS,
            name="update",
        )

    estimate = start_image
    outgoing = pick(ids, table, start_image)
    for iteration in range(ITERATIONS):
        own, *partial, residual = apply_model(
            places, block_rows, model_blocks, measured, *exchange(outgoing)
        )
        received = [swap(piece, "chan", chan_count, d) for d, piece in enumerate(partial, 1)]
        totals = reduce_parts(own, *received)
        pieces = exchange(totals)
        returned = jnp.concatenate([pieces[array][i] for array, i in where.values()])
        spread = [swap(returned, "chan", chan_count, d) for d in range(chan_count)]
        estimate, *outgoing = update(iteration == ITERATIONS - 1)(
            ids, table, gains, estimate, *spread
        )
    return (estimate, residual)


def solution(mesh):
    in_specs = (
        P(("vox", "chan"), None, None),
        P("vox", None, None),
        P(("vox", "chan"), None, None),
        P(),
        P("vox", None, None),
        P(("vox", "chan")),
        P(("vox", "chan")),
    )
    out_specs = (P("vox", None, None), P(("vox", "chan"), None, None))
    return jax.shard_map(shards, mesh=mesh, in_specs=in_specs, out_specs=out_specs, check_vma=False)
```

```python
import functools

import jax
import jax.numpy as jnp
from jax import lax
from jax.experimental import pallas as pl
from jax.experimental.pallas import tpu as pltpu
from jax.sharding import PartitionSpec as P

ITERATIONS = 4


VMEM = pl.BlockSpec(memory_space=pltpu.VMEM)
SMEM = pl.BlockSpec(memory_space=pltpu.SMEM)
PARAMS = pltpu.CompilerParams(vmem_limit_bytes=32 * 1024 * 1024)


def model_kernel(slots, places, rows, model, measured, tiles, own, *refs):
    *sent, residual, narrow, sums = refs
    wide = own.shape[0]
    count = model.shape[0]
    residual[...] = measured[...]
    sums[...] = jnp.zeros_like(sums)
    for k in range(count):
        part = lax.dot_general(
            tiles[slots[k]],
            model[k],
            (((1,), (1,)), ((), ())),
            preferred_element_type=jnp.float32,
        )
        residual[rows[k]] -= part
    narrow[...] = residual[...].astype(jnp.bfloat16)
    for k in range(count):
        part = jnp.dot(narrow[rows[k]], model[k], preferred_element_type=jnp.float32)
        sums[places[k]] += part
    own[...] = sums[:wide]
    for d, out in enumerate(sent, 1):
        out[...] = sums[d * wide : (d + 1) * wide].astype(jnp.bfloat16)


def reduce_kernel(own, *refs):
    *received, out = refs
    total = own[...]
    for piece in received:
        total = total + piece[...].astype(jnp.float32)
    out[...] = total.astype(jnp.bfloat16)


def pick_kernel(table, image, out):
    vox_count, capacity = table.shape
    for v in range(vox_count):
        for s in range(capacity):
            tile = jnp.maximum(table[v, s], 0)
            out[v * capacity + s] = image[tile].astype(jnp.bfloat16)


def update_kernel(chan_count, ids, table, gains, image, *refs):
    received = refs[:chan_count]
    estimate, *outs = refs[chan_count:-1]
    gradient = refs[-1]
    vox_count, capacity = table.shape
    per = capacity // chan_count
    gradient[...] = jnp.zeros_like(gradient)
    for d in range(chan_count):
        first = (ids[0] ^ d) * per
        for v in range(vox_count):
            for p in range(per):
                tile = jnp.maximum(table[v, first + p], 0)
                gradient[tile] += received[d][v * per + p].astype(jnp.float32)
    estimate[...] = jnp.maximum(image[...] + gains[...][None] * gradient[...], 0.0)
    if outs:
        pick_kernel(table, estimate, *outs)


def shards(model_blocks, start_image, measured, step_size, sent_tiles, block_rows, block_slots):
    vox_count = lax.axis_size("vox")
    chan_count = lax.axis_size("chan")
    chan = lax.axis_index("chan")
    table = sent_tiles[0]
    capacity = table.shape[1]
    per = capacity // chan_count
    tile_count, wave_count, width = start_image.shape
    row_count = measured.shape[0]
    slot_count = vox_count * capacity
    wide = vox_count * per
    tile = (wave_count, width)
    ids = chan.astype(jnp.int32)[None]
    slab, slot = block_slots // capacity, block_slots % capacity
    places = (((slot // per) ^ chan) * vox_count + slab) * per + slot % per
    gains = jnp.broadcast_to(step_size[:, None], tile)

    def shape(count, dtype):
        return jax.ShapeDtypeStruct((count, *tile), dtype)

    def swap(array, step):
        pairs = [(i, i ^ step) for i in range(chan_count)]
        return lax.ppermute(array, "chan", pairs) if step else array

    def exchange(array):
        return lax.all_to_all(array, "vox", split_axis=0, concat_axis=0, tiled=True)

    apply_model = pl.pallas_call(
        model_kernel,
        out_shape=(
            shape(wide, jnp.float32),
            *[shape(wide, jnp.bfloat16)] * (chan_count - 1),
            shape(row_count, jnp.float32),
        ),
        in_specs=[SMEM, SMEM, SMEM, VMEM, VMEM, VMEM],
        out_specs=[VMEM] * (chan_count + 1),
        scratch_shapes=[
            pltpu.VMEM((row_count, *tile), jnp.bfloat16),
            pltpu.VMEM((slot_count, *tile), jnp.float32),
        ],
        compiler_params=PARAMS,
        name="model",
    )
    reduce_parts = pl.pallas_call(
        reduce_kernel,
        out_shape=shape(wide, jnp.bfloat16),
        in_specs=[VMEM] * chan_count,
        out_specs=VMEM,
        compiler_params=PARAMS,
        name="reduce",
    )
    pick = pl.pallas_call(
        pick_kernel,
        out_shape=shape(slot_count, jnp.bfloat16),
        in_specs=[SMEM, VMEM],
        out_specs=VMEM,
        compiler_params=PARAMS,
        name="pick",
    )

    def update(last):
        outs = [] if last else [shape(slot_count, jnp.bfloat16)]
        return pl.pallas_call(
            functools.partial(update_kernel, chan_count),
            out_shape=[shape(tile_count, jnp.float32)] + outs,
            in_specs=[SMEM, SMEM, VMEM, VMEM] + [VMEM] * chan_count,
            out_specs=[VMEM] * (len(outs) + 1),
            scratch_shapes=[pltpu.VMEM((tile_count, *tile), jnp.float32)],
            compiler_params=PARAMS,
            name="update",
        )

    estimate = start_image
    outgoing = [pick(table, start_image)]
    for iteration in range(ITERATIONS):
        tiles = exchange(*outgoing)
        own, *partial, residual = apply_model(
            block_slots, places, block_rows, model_blocks, measured, tiles
        )
        total = reduce_parts(own, *[swap(piece, d) for d, piece in enumerate(partial, 1)])
        returned = exchange(total)
        spread = [swap(returned, d) for d in range(chan_count)]
        estimate, *outgoing = update(iteration == ITERATIONS - 1)(
            ids, table, gains, estimate, *spread
        )
    return (estimate, residual)


def solution(mesh):
    in_specs = (
        P(("vox", "chan"), None, None),
        P("vox", None, None),
        P(("vox", "chan"), None, None),
        P(),
        P("vox", None, None),
        P(("vox", "chan")),
        P(("vox", "chan")),
    )
    out_specs = (P("vox", None, None), P(("vox", "chan"), None, None))
    return jax.shard_map(shards, mesh=mesh, in_specs=in_specs, out_specs=out_specs, check_vma=False)
```

```python
import functools

import jax
import jax.numpy as jnp
from jax import lax
from jax.experimental import pallas as pl
from jax.experimental.pallas import tpu as pltpu
from jax.sharding import PartitionSpec as P

ITERATIONS = 4


VMEM = pl.BlockSpec(memory_space=pltpu.VMEM)
SMEM = pl.BlockSpec(memory_space=pltpu.SMEM)
PARAMS = pltpu.CompilerParams(vmem_limit_bytes=32 * 1024 * 1024)


def model_kernel(chan_count, places, rows, model, measured, *refs):
    arrived = refs[:chan_count]
    own, *sent = refs[chan_count : 2 * chan_count]
    residual, tiles, narrow, sums = refs[2 * chan_count :]
    wide = own.shape[0]
    count = model.shape[0]
    for d, piece in enumerate(arrived):
        tiles[d * wide : (d + 1) * wide] = piece[...]
    residual[...] = measured[...]
    sums[...] = jnp.zeros_like(sums)
    for k in range(count):
        part = lax.dot_general(
            tiles[places[k]],
            model[k],
            (((1,), (1,)), ((), ())),
            preferred_element_type=jnp.float32,
        )
        residual[rows[k]] -= part
    narrow[...] = residual[...].astype(jnp.bfloat16)
    for k in range(count):
        part = jnp.dot(narrow[rows[k]], model[k], preferred_element_type=jnp.float32)
        sums[places[k]] += part
    own[...] = sums[:wide]
    for d, out in enumerate(sent, 1):
        out[...] = sums[d * wide : (d + 1) * wide].astype(jnp.bfloat16)


def reduce_kernel(share, own, *refs):
    received, outs = refs[:-share], refs[-share:]
    total = own[...]
    for piece in received:
        total = total + piece[...].astype(jnp.float32)
    capacity = total.shape[0] // share
    for r, out in enumerate(outs):
        out[...] = total[r * capacity : (r + 1) * capacity].astype(jnp.bfloat16)


def tile_of(ids, table, share, d, r, s):
    return jnp.maximum(table[ids[0] ^ ((ids[1] ^ d) * share + r), s], 0)


def pick_kernel(ids, table, image, *outs):
    for r, out in enumerate(outs):
        for s in range(table.shape[1]):
            tile = tile_of(ids, table, len(outs), 0, r, s)
            out[s] = image[tile].astype(jnp.bfloat16)


def update_kernel(chan_count, ids, table, gains, image, *refs):
    received = refs[:chan_count]
    estimate, *outs = refs[chan_count:-1]
    gradient = refs[-1]
    vox_count, capacity = table.shape
    share = vox_count // chan_count
    gradient[...] = jnp.zeros_like(gradient)
    for d in range(chan_count):
        for r in range(share):
            for s in range(capacity):
                tile = tile_of(ids, table, share, d, r, s)
                gradient[tile] += received[d][r * capacity + s].astype(jnp.float32)
    estimate[...] = jnp.maximum(image[...] + gains[...][None] * gradient[...], 0.0)
    if outs:
        pick_kernel(ids, table, estimate, *outs)


def shards(model_blocks, start_image, measured, step_size, sent_tiles, block_rows, block_slots):
    vox_count = lax.axis_size("vox")
    chan_count = lax.axis_size("chan")
    vox, chan = lax.axis_index("vox"), lax.axis_index("chan")
    table = sent_tiles[0]
    capacity = table.shape[1]
    share = vox_count // chan_count
    tile_count, wave_count, width = start_image.shape
    row_count = measured.shape[0]
    slot_count = vox_count * capacity
    wide = share * capacity
    tile = (wave_count, width)
    ids = jnp.stack([vox, chan]).astype(jnp.int32)
    partner, slot = (block_slots // capacity) ^ vox, block_slots % capacity
    places = (((partner // share) ^ chan) * share + partner % share) * capacity + slot
    gains = jnp.broadcast_to(step_size[:, None], tile)

    def shape(count, dtype):
        return jax.ShapeDtypeStruct((count, *tile), dtype)

    def swap(array, d):
        pairs = [(i, i ^ d) for i in range(chan_count)]
        return lax.ppermute(array, "chan", pairs) if d else array

    def exchange(pieces):
        arrived = []
        for r, piece in enumerate(pieces):
            pairs = [
                (v * chan_count + c, (v ^ (c * share + r)) * chan_count + c)
                for v in range(vox_count)
                for c in range(chan_count)
            ]
            arrived.append(lax.ppermute(piece, ("vox", "chan"), pairs))
        joined = jnp.concatenate(arrived)
        return [swap(joined, d) for d in range(chan_count)]

    apply_model = pl.pallas_call(
        functools.partial(model_kernel, chan_count),
        out_shape=(
            shape(wide, jnp.float32),
            *[shape(wide, jnp.bfloat16)] * (chan_count - 1),
            shape(row_count, jnp.float32),
        ),
        in_specs=[SMEM, SMEM, VMEM, VMEM] + [VMEM] * chan_count,
        out_specs=[VMEM] * (chan_count + 1),
        scratch_shapes=[
            pltpu.VMEM((slot_count, *tile), jnp.bfloat16),
            pltpu.VMEM((row_count, *tile), jnp.bfloat16),
            pltpu.VMEM((slot_count, *tile), jnp.float32),
        ],
        compiler_params=PARAMS,
        name="model",
    )
    reduce_parts = pl.pallas_call(
        functools.partial(reduce_kernel, share),
        out_shape=[shape(capacity, jnp.bfloat16)] * share,
        in_specs=[VMEM] * chan_count,
        out_specs=[VMEM] * share,
        compiler_params=PARAMS,
        name="reduce",
    )
    pick = pl.pallas_call(
        pick_kernel,
        out_shape=[shape(capacity, jnp.bfloat16)] * share,
        in_specs=[SMEM, SMEM, VMEM],
        out_specs=[VMEM] * share,
        compiler_params=PARAMS,
        name="pick",
    )

    def update(last):
        outs = [] if last else [shape(capacity, jnp.bfloat16)] * share
        return pl.pallas_call(
            functools.partial(update_kernel, chan_count),
            out_shape=[shape(tile_count, jnp.float32)] + outs,
            in_specs=[SMEM, SMEM, VMEM, VMEM] + [VMEM] * chan_count,
            out_specs=[VMEM] * (len(outs) + 1),
            scratch_shapes=[pltpu.VMEM((tile_count, *tile), jnp.float32)],
            compiler_params=PARAMS,
            name="update",
        )

    estimate = start_image
    outgoing = pick(ids, table, start_image)
    for iteration in range(ITERATIONS):
        own, *partial, residual = apply_model(
            places, block_rows, model_blocks, measured, *exchange(outgoing)
        )
        totals = reduce_parts(own, *[swap(piece, d) for d, piece in enumerate(partial, 1)])
        estimate, *outgoing = update(iteration == ITERATIONS - 1)(
            ids, table, gains, estimate, *exchange(totals)
        )
    return (estimate, residual)


def solution(mesh):
    in_specs = (
        P(("vox", "chan"), None, None),
        P("vox", None, None),
        P(("vox", "chan"), None, None),
        P(),
        P("vox", None, None),
        P(("vox", "chan")),
        P(("vox", "chan")),
    )
    out_specs = (P("vox", None, None), P(("vox", "chan"), None, None))
    return jax.shard_map(shards, mesh=mesh, in_specs=in_specs, out_specs=out_specs, check_vma=False)
```

```python
import functools
import math

import jax
import jax.numpy as jnp
from jax import lax
from jax.experimental import pallas as pl
from jax.experimental.pallas import tpu as pltpu
from jax.sharding import Mesh, PartitionSpec as P

ITERATIONS = 4


VMEM = pl.BlockSpec(memory_space=pltpu.VMEM)
SMEM = pl.BlockSpec(memory_space=pltpu.SMEM)
PARAMS = pltpu.CompilerParams(vmem_limit_bytes=32 * 1024 * 1024)


def model_kernel(index, model, measured, tiles, own, *refs):
    *sent, residual, narrow, sums = refs
    wide = own.shape[0]
    count = model.shape[0]
    residual[...] = measured[...]
    sums[...] = jnp.zeros_like(sums)
    for k in range(count):
        part = lax.dot_general(
            tiles[index[0, k]],
            model[k],
            (((1,), (1,)), ((), ())),
            preferred_element_type=jnp.float32,
        )
        residual[index[2, k]] -= part
    narrow[...] = residual[...].astype(jnp.bfloat16)
    for k in range(count):
        part = jnp.dot(narrow[index[2, k]], model[k], preferred_element_type=jnp.float32)
        sums[index[1, k]] += part
    own[...] = sums[:wide]
    for d, out in enumerate(sent, 1):
        out[...] = sums[d * wide : (d + 1) * wide].astype(jnp.bfloat16)


def stage_kernel(*refs):
    *pairs, sems = refs
    half = len(pairs) // 2
    copies = [
        pltpu.make_async_copy(pairs[i], pairs[half + i], sems.at[i]) for i in range(half)
    ]
    for copy in copies:
        copy.start()
    for copy in copies:
        copy.wait()


def reduce_kernel(own, *refs):
    *received, out = refs
    vox_count, hi_count, per = out.shape[:3]
    total = own[...]
    for piece in received:
        total = total + piece[...].astype(jnp.float32)
    total = total.astype(jnp.bfloat16)
    for v in range(vox_count):
        for h in range(hi_count):
            out[v, h] = total[v * per : (v + 1) * per]


def merge_kernel(parts, out):
    vox_count, hi_count, per = parts.shape[:3]
    for v in range(vox_count):
        total = parts[v, 0].astype(jnp.float32)
        for h in range(1, hi_count):
            total = total + parts[v, h].astype(jnp.float32)
        out[v * per : (v + 1) * per] = total.astype(jnp.bfloat16)


def pick_kernel(table, image, out):
    vox_count, capacity = table.shape
    for v in range(vox_count):
        for s in range(capacity):
            tile = jnp.maximum(table[v, s], 0)
            out[v * capacity + s] = image[tile].astype(jnp.bfloat16)


def update_kernel(lo_count, ids, table, gains, image, *refs):
    received = refs[:lo_count]
    estimate, *outs = refs[lo_count:-1]
    gradient = refs[-1]
    vox_count, capacity = table.shape
    per = capacity // lo_count
    gradient[...] = jnp.zeros_like(gradient)
    for d in range(lo_count):
        first = (ids[0] ^ d) * per
        for v in range(vox_count):
            for p in range(per):
                tile = jnp.maximum(table[v, first + p], 0)
                gradient[tile] += received[d][v * per + p].astype(jnp.float32)
    estimate[...] = jnp.maximum(image[...] + gains[...][None] * gradient[...], 0.0)
    if outs:
        pick_kernel(table, estimate, *outs)


def shards(model_blocks, start_image, measured, step_size, sent_tiles, block_rows, block_slots):
    vox_count = lax.axis_size("vox")
    hi_count = lax.axis_size("hi")
    lo_count = lax.axis_size("lo")
    lo = lax.axis_index("lo")
    table = sent_tiles[0]
    capacity = table.shape[1]
    per = capacity // lo_count
    tile_count, wave_count, width = start_image.shape
    row_count = measured.shape[0]
    slot_count = vox_count * capacity
    wide = vox_count * per
    tile = (wave_count, width)
    ids = lo.astype(jnp.int32)[None]
    slab, slot = block_slots // capacity, block_slots % capacity
    places = (((slot // per) ^ lo) * vox_count + slab) * per + slot % per
    index = jnp.stack([block_slots, places, block_rows])
    gains = jnp.broadcast_to(step_size[:, None], tile)

    def shape(count, dtype):
        return jax.ShapeDtypeStruct((count, *tile), dtype)

    def swap(array, d):
        pairs = [(i, i ^ d) for i in range(lo_count)]
        return lax.ppermute(array, "lo", pairs) if d else array

    def exchange(array, axes):
        return lax.all_to_all(array, axes, split_axis=0, concat_axis=0, tiled=True)

    stage = pl.pallas_call(
        stage_kernel,
        out_shape=[
            jax.ShapeDtypeStruct(model_blocks.shape, model_blocks.dtype),
            jax.ShapeDtypeStruct(measured.shape, measured.dtype),
        ],
        in_specs=[pl.BlockSpec(memory_space=pltpu.HBM)] * 2,
        out_specs=[VMEM] * 2,
        scratch_shapes=[pltpu.SemaphoreType.DMA((2,))],
        compiler_params=PARAMS,
        cost_estimate=pl.CostEstimate(
            flops=0, bytes_accessed=2 * model_blocks.size * 2, transcendentals=0
        ),
        name="stage",
    )
    apply_model = pl.pallas_call(
        model_kernel,
        out_shape=(
            shape(wide, jnp.float32),
            *[shape(wide, jnp.bfloat16)] * (lo_count - 1),
            shape(row_count, jnp.float32),
        ),
        in_specs=[SMEM, VMEM, VMEM, VMEM],
        out_specs=[VMEM] * (lo_count + 1),
        scratch_shapes=[
            pltpu.VMEM((row_count, *tile), jnp.bfloat16),
            pltpu.VMEM((slot_count, *tile), jnp.float32),
        ],
        compiler_params=PARAMS,
        name="model",
    )
    reduce_parts = pl.pallas_call(
        reduce_kernel,
        out_shape=jax.ShapeDtypeStruct((vox_count, hi_count, per, *tile), jnp.bfloat16),
        in_specs=[VMEM] * lo_count,
        out_specs=VMEM,
        compiler_params=PARAMS,
        name="reduce",
    )
    merge = pl.pallas_call(
        merge_kernel,
        out_shape=shape(wide, jnp.bfloat16),
        in_specs=[VMEM],
        out_specs=VMEM,
        compiler_params=PARAMS,
        name="merge",
    )
    pick = pl.pallas_call(
        pick_kernel,
        out_shape=shape(slot_count, jnp.bfloat16),
        in_specs=[SMEM, VMEM],
        out_specs=VMEM,
        compiler_params=PARAMS,
        name="pick",
    )

    def update(last):
        outs = [] if last else [shape(slot_count, jnp.bfloat16)]
        return pl.pallas_call(
            functools.partial(update_kernel, lo_count),
            out_shape=[shape(tile_count, jnp.float32)] + outs,
            in_specs=[SMEM, SMEM, VMEM, VMEM] + [VMEM] * lo_count,
            out_specs=[VMEM] * (len(outs) + 1),
            scratch_shapes=[pltpu.VMEM((tile_count, *tile), jnp.float32)],
            compiler_params=PARAMS,
            name="update",
        )

    estimate = start_image
    outgoing = [pick(table, start_image)]
    model, signals = stage(model_blocks, measured)
    for iteration in range(ITERATIONS):
        tiles = exchange(*outgoing, "vox")
        own, *partial, residual = apply_model(index, model, signals, tiles)
        total = reduce_parts(own, *[swap(piece, d) for d, piece in enumerate(partial, 1)])
        total = total.reshape(vox_count * hi_count, per, *tile)
        parts = exchange(total, ("vox", "hi"))
        merged = merge(parts.reshape(vox_count, hi_count, per, *tile))
        estimate, *outgoing = update(iteration == ITERATIONS - 1)(
            ids, table, gains, estimate, *[swap(merged, d) for d in range(lo_count)]
        )
    return (estimate, residual)


def solution(mesh):
    vox_count, chan_count = mesh.devices.shape
    lo_count = math.gcd(chan_count, 2)
    cut = Mesh(
        mesh.devices.reshape(vox_count, chan_count // lo_count, lo_count), ("vox", "hi", "lo")
    )
    everywhere = ("vox", "hi", "lo")
    in_specs = (
        P(everywhere, None, None),
        P("vox", None, None),
        P(everywhere, None, None),
        P(),
        P("vox", None, None),
        P(everywhere),
        P(everywhere),
    )
    out_specs = (P("vox", None, None), P(everywhere, None, None))
    return jax.shard_map(shards, mesh=cut, in_specs=in_specs, out_specs=out_specs, check_vma=False)
```

```python
import functools
import math

import jax
import jax.numpy as jnp
from jax import lax
from jax.experimental import pallas as pl
from jax.experimental.pallas import tpu as pltpu
from jax.sharding import Mesh, PartitionSpec as P

ITERATIONS = 4


VMEM = pl.BlockSpec(memory_space=pltpu.VMEM)
SMEM = pl.BlockSpec(memory_space=pltpu.SMEM)
PARAMS = pltpu.CompilerParams(vmem_limit_bytes=32 * 1024 * 1024)


def grouped(source, index, column, model, k, size, dims):
    left = [source[index[column, k + i]] for i in range(size)]
    blocks = [model[k + i] for i in range(size)]
    if size < 4:
        return [
            lax.dot_general(x, block, dims, preferred_element_type=jnp.float32)
            for x, block in zip(left, blocks)
        ]
    zero = jnp.zeros_like(left[0])
    rows = jnp.concatenate(
        [
            jnp.concatenate([x, zero] if i % 2 == 0 else [zero, x], axis=1)
            for i, x in enumerate(left)
        ],
        axis=0,
    )
    depth = dims[0][1][0]
    halves = [jnp.concatenate(blocks[n : n + 2], axis=depth) for n in (0, 2)]
    whole = jnp.concatenate(halves, axis=1 - depth)
    out = lax.dot_general(rows, whole, dims, preferred_element_type=jnp.float32)
    height, width = left[0].shape[0], out.shape[1] // 2
    return [
        out[i * height : (i + 1) * height, i // 2 * width : (i // 2 + 1) * width]
        for i in range(4)
    ]


def model_kernel(index, model, measured, tiles, own, *refs):
    *sent, residual, narrow, sums = refs
    wide = own.shape[0]
    count = model.shape[0]
    residual[...] = measured[...]
    sums[...] = jnp.zeros_like(sums)
    for k in range(0, count, 4):
        for i, part in enumerate(
            grouped(tiles, index, 0, model, k, min(4, count - k), (((1,), (1,)), ((), ())))
        ):
            residual[index[2, k + i]] -= part
    narrow[...] = residual[...].astype(jnp.bfloat16)
    for k in range(0, count, 4):
        for i, part in enumerate(
            grouped(narrow, index, 2, model, k, min(4, count - k), (((1,), (0,)), ((), ())))
        ):
            sums[index[1, k + i]] += part
    own[...] = sums[:wide]
    for d, out in enumerate(sent, 1):
        out[...] = sums[d * wide : (d + 1) * wide].astype(jnp.bfloat16)


def stage_kernel(*refs):
    *pairs, sems = refs
    half = len(pairs) // 2
    copies = [
        pltpu.make_async_copy(pairs[i], pairs[half + i], sems.at[i]) for i in range(half)
    ]
    for copy in copies:
        copy.start()
    for copy in copies:
        copy.wait()


def reduce_kernel(own, *refs):
    *received, out = refs
    vox_count, hi_count, per = out.shape[:3]
    total = own[...]
    for piece in received:
        total = total + piece[...].astype(jnp.float32)
    total = total.astype(jnp.bfloat16)
    for v in range(vox_count):
        for h in range(hi_count):
            out[v, h] = total[v * per : (v + 1) * per]


def merge_kernel(parts, out):
    vox_count, hi_count, per = parts.shape[:3]
    for v in range(vox_count):
        total = parts[v, 0].astype(jnp.float32)
        for h in range(1, hi_count):
            total = total + parts[v, h].astype(jnp.float32)
        out[v * per : (v + 1) * per] = total.astype(jnp.bfloat16)


def pick_kernel(table, image, out):
    _, vox_count, capacity = table.shape
    for v in range(vox_count):
        for s in range(capacity):
            tile = jnp.maximum(table[0, v, s], 0)
            out[v * capacity + s] = image[tile].astype(jnp.bfloat16)


def update_kernel(lo_count, ids, table, gains, image, *refs):
    received = refs[:lo_count]
    estimate, *outs = refs[lo_count:-1]
    gradient = refs[-1]
    _, vox_count, capacity = table.shape
    per = capacity // lo_count
    gradient[...] = jnp.zeros_like(gradient)
    for d in range(lo_count):
        first = (ids[0] ^ d) * per
        for v in range(vox_count):
            for p in range(per):
                tile = jnp.maximum(table[0, v, first + p], 0)
                gradient[tile] += received[d][v * per + p].astype(jnp.float32)
    estimate[...] = jnp.maximum(image[...] + gains[...][None] * gradient[...], 0.0)
    if outs:
        pick_kernel(table, estimate, *outs)


def shards(model_blocks, start_image, measured, step_size, sent_tiles, block_rows, block_slots):
    vox_count = lax.axis_size("vox")
    hi_count = lax.axis_size("hi")
    lo_count = lax.axis_size("lo")
    lo = lax.axis_index("lo")
    capacity = sent_tiles.shape[2]
    per = capacity // lo_count
    tile_count, wave_count, width = start_image.shape
    row_count = measured.shape[0]
    slot_count = vox_count * capacity
    wide = vox_count * per
    tile = (wave_count, width)
    ids = lo.astype(jnp.int32)[None]
    slab, slot = block_slots // capacity, block_slots % capacity
    places = (((slot // per) ^ lo) * vox_count + slab) * per + slot % per
    index = jnp.stack([block_slots, places, block_rows])
    gains = jnp.broadcast_to(step_size[:, None], tile)

    def shape(count, dtype):
        return jax.ShapeDtypeStruct((count, *tile), dtype)

    def swap(array, d):
        pairs = [(i, i ^ d) for i in range(lo_count)]
        return lax.ppermute(array, "lo", pairs) if d else array

    def exchange(array, axes):
        return lax.all_to_all(array, axes, split_axis=0, concat_axis=0, tiled=True)

    stage = pl.pallas_call(
        stage_kernel,
        out_shape=[
            jax.ShapeDtypeStruct(model_blocks.shape, model_blocks.dtype),
            jax.ShapeDtypeStruct(measured.shape, measured.dtype),
        ],
        in_specs=[pl.BlockSpec(memory_space=pltpu.HBM)] * 2,
        out_specs=[VMEM] * 2,
        scratch_shapes=[pltpu.SemaphoreType.DMA((2,))],
        compiler_params=PARAMS,
        cost_estimate=pl.CostEstimate(
            flops=0, bytes_accessed=2 * model_blocks.size * 2, transcendentals=0
        ),
        name="stage",
    )
    apply_model = pl.pallas_call(
        model_kernel,
        out_shape=(
            shape(wide, jnp.float32),
            *[shape(wide, jnp.bfloat16)] * (lo_count - 1),
            shape(row_count, jnp.float32),
        ),
        in_specs=[SMEM, VMEM, VMEM, VMEM],
        out_specs=[VMEM] * (lo_count + 1),
        scratch_shapes=[
            pltpu.VMEM((row_count, *tile), jnp.bfloat16),
            pltpu.VMEM((slot_count, *tile), jnp.float32),
        ],
        compiler_params=PARAMS,
        name="model",
    )
    reduce_parts = pl.pallas_call(
        reduce_kernel,
        out_shape=jax.ShapeDtypeStruct((vox_count, hi_count, per, *tile), jnp.bfloat16),
        in_specs=[VMEM] * lo_count,
        out_specs=VMEM,
        compiler_params=PARAMS,
        name="reduce",
    )
    merge = pl.pallas_call(
        merge_kernel,
        out_shape=shape(wide, jnp.bfloat16),
        in_specs=[VMEM],
        out_specs=VMEM,
        compiler_params=PARAMS,
        name="merge",
    )
    pick = pl.pallas_call(
        pick_kernel,
        out_shape=shape(slot_count, jnp.bfloat16),
        in_specs=[SMEM, VMEM],
        out_specs=VMEM,
        compiler_params=PARAMS,
        name="pick",
    )

    def update(last):
        outs = [] if last else [shape(slot_count, jnp.bfloat16)]
        return pl.pallas_call(
            functools.partial(update_kernel, lo_count),
            out_shape=[shape(tile_count, jnp.float32)] + outs,
            in_specs=[SMEM, SMEM, VMEM, VMEM] + [VMEM] * lo_count,
            out_specs=[VMEM] * (len(outs) + 1),
            scratch_shapes=[pltpu.VMEM((tile_count, *tile), jnp.float32)],
            compiler_params=PARAMS,
            name="update",
        )

    estimate = start_image
    outgoing = [pick(sent_tiles, start_image)]
    model, signals = stage(model_blocks, measured)
    for iteration in range(ITERATIONS):
        tiles = exchange(*outgoing, "vox")
        own, *partial, residual = apply_model(index, model, signals, tiles)
        total = reduce_parts(own, *[swap(piece, d) for d, piece in enumerate(partial, 1)])
        total = total.reshape(vox_count * hi_count, per, *tile)
        parts = exchange(total, ("vox", "hi"))
        merged = merge(parts.reshape(vox_count, hi_count, per, *tile))
        estimate, *outgoing = update(iteration == ITERATIONS - 1)(
            ids, sent_tiles, gains, estimate, *[swap(merged, d) for d in range(lo_count)]
        )
    return (estimate, residual)


def solution(mesh):
    vox_count, chan_count = mesh.devices.shape
    lo_count = math.gcd(chan_count, 2)
    cut = Mesh(
        mesh.devices.reshape(vox_count, chan_count // lo_count, lo_count), ("vox", "hi", "lo")
    )
    everywhere = ("vox", "hi", "lo")
    in_specs = (
        P(everywhere, None, None),
        P("vox", None, None),
        P(everywhere, None, None),
        P(),
        P("vox", None, None),
        P(everywhere),
        P(everywhere),
    )
    out_specs = (P("vox", None, None), P(everywhere, None, None))
    return jax.shard_map(shards, mesh=cut, in_specs=in_specs, out_specs=out_specs, check_vma=False)
```

```python
import functools
import math

import jax
import jax.numpy as jnp
from jax import lax
from jax.experimental import pallas as pl
from jax.experimental.pallas import tpu as pltpu
from jax.sharding import Mesh, PartitionSpec as P

ITERATIONS = 4


VMEM = pl.BlockSpec(memory_space=pltpu.VMEM)
SMEM = pl.BlockSpec(memory_space=pltpu.SMEM)
PARAMS = pltpu.CompilerParams(vmem_limit_bytes=32 * 1024 * 1024)


def grouped(source, index, column, d, model, k, size, dims):
    left = [source[index[d, column, k + i]] for i in range(size)]
    blocks = [model[k + i] for i in range(size)]
    if size < 4:
        return [
            lax.dot_general(x, block, dims, preferred_element_type=jnp.float32)
            for x, block in zip(left, blocks)
        ]
    zero = jnp.zeros_like(left[0])
    rows = jnp.concatenate(
        [
            jnp.concatenate([x, zero] if i % 2 == 0 else [zero, x], axis=1)
            for i, x in enumerate(left)
        ],
        axis=0,
    )
    depth = dims[0][1][0]
    halves = [jnp.concatenate(blocks[n : n + 2], axis=depth) for n in (0, 2)]
    whole = jnp.concatenate(halves, axis=1 - depth)
    out = lax.dot_general(rows, whole, dims, preferred_element_type=jnp.float32)
    height, width = left[0].shape[0], out.shape[1] // 2
    return [
        out[i * height : (i + 1) * height, i // 2 * width : (i // 2 + 1) * width]
        for i in range(4)
    ]


def model_kernel(lo_count, index, measured, tiles, *refs):
    models = refs[:lo_count]
    out, residual, narrow, sums = refs[lo_count:]
    vox_count, hi_count, capacity = out.shape[:3]
    count = models[0].shape[0]
    residual[...] = measured[...]
    sums[...] = jnp.zeros_like(sums)
    for d, model in enumerate(models):
        for k in range(0, count, 4):
            for i, part in enumerate(
                grouped(
                    tiles, index, 0, d, model, k, min(4, count - k), (((1,), (1,)), ((), ()))
                )
            ):
                residual[index[d, 1, k + i]] -= part
    narrow[...] = residual[...].astype(jnp.bfloat16)
    for d, model in enumerate(models):
        for k in range(0, count, 4):
            for i, part in enumerate(
                grouped(
                    narrow, index, 1, d, model, k, min(4, count - k), (((1,), (0,)), ((), ()))
                )
            ):
                sums[index[d, 0, k + i]] += part
    for v in range(vox_count):
        piece = sums[v * capacity : (v + 1) * capacity].astype(jnp.bfloat16)
        for h in range(hi_count):
            out[v, h] = piece


def stage_kernel(*refs):
    *pairs, sems = refs
    half = len(pairs) // 2
    copies = [
        pltpu.make_async_copy(pairs[i], pairs[half + i], sems.at[i]) for i in range(half)
    ]
    for copy in copies:
        copy.start()
    for copy in copies:
        copy.wait()


def pick_tiles(table, image, out):
    _, vox_count, capacity = table.shape
    for v in range(vox_count):
        for s in range(capacity):
            tile = jnp.maximum(table[0, v, s], 0)
            out[v * capacity + s] = image[tile].astype(jnp.bfloat16)


def part_of(lo, size):
    return (slice(None), pl.ds(pl.multiple_of(lo * size, size), size))


def pick_kernel(lo, table, image, part, out):
    part[...] = image[part_of(lo[0], part.shape[1])]
    pick_tiles(table, part, out)


def update_kernel(table, gains, image, parts, estimate, *refs):
    *outs, gradient = refs
    vox_count, hi_count, capacity = parts.shape[:3]
    gradient[...] = jnp.zeros_like(gradient)
    for v in range(vox_count):
        for s in range(capacity):
            tile = jnp.maximum(table[0, v, s], 0)
            total = parts[v, 0, s].astype(jnp.float32)
            for h in range(1, hi_count):
                total = total + parts[v, h, s].astype(jnp.float32)
            gradient[tile] += total
    estimate[...] = jnp.maximum(image[...] + gains[...][None] * gradient[...], 0.0)
    if outs:
        pick_tiles(table, estimate, *outs)


def join_kernel(lo, *refs):
    *parts, out = refs
    for d, part in enumerate(parts):
        out[part_of(lo[0] ^ d, part.shape[1])] = part[...]


def shards(model_blocks, start_image, measured, step_size, sent_tiles, block_rows, block_slots):
    vox_count = lax.axis_size("vox")
    hi_count = lax.axis_size("hi")
    lo_count = lax.axis_size("lo")
    lo = lax.axis_index("lo")
    capacity = sent_tiles.shape[2]
    tile_count, wave_count, width = start_image.shape
    row_count = measured.shape[0]
    slot_count = vox_count * capacity
    waves = wave_count // lo_count
    tile = (waves, width)
    ids = lo.astype(jnp.int32)[None]

    def shape(count, dtype):
        return jax.ShapeDtypeStruct((count, *tile), dtype)

    def swap(array, d):
        pairs = [(i, i ^ d) for i in range(lo_count)]
        return lax.ppermute(array, "lo", pairs) if d else array

    def exchange(array, axes):
        return lax.all_to_all(array, axes, split_axis=0, concat_axis=0, tiled=True)

    def call(kernel, out_shape, in_specs, scratch, name, **options):
        return pl.pallas_call(
            kernel,
            out_shape=out_shape,
            in_specs=in_specs,
            out_specs=[VMEM] * len(out_shape),
            scratch_shapes=scratch,
            compiler_params=PARAMS,
            name=name,
            **options,
        )

    pick = call(
        pick_kernel,
        [shape(tile_count, jnp.float32), shape(slot_count, jnp.bfloat16)],
        [SMEM, SMEM, VMEM],
        [],
        "pick",
    )
    stage = call(
        stage_kernel,
        [jax.ShapeDtypeStruct(model_blocks.shape, model_blocks.dtype)] * lo_count,
        [pl.BlockSpec(memory_space=pltpu.HBM)] * lo_count,
        [pltpu.SemaphoreType.DMA((lo_count,))],
        "stage",
        cost_estimate=pl.CostEstimate(
            flops=0, bytes_accessed=4 * lo_count * model_blocks.size, transcendentals=0
        ),
    )
    apply_model = call(
        functools.partial(model_kernel, lo_count),
        [
            jax.ShapeDtypeStruct((vox_count, hi_count, capacity, *tile), jnp.bfloat16),
            shape(lo_count * row_count, jnp.float32),
        ],
        [SMEM, VMEM, VMEM] + [VMEM] * lo_count,
        [
            pltpu.VMEM((lo_count * row_count, *tile), jnp.bfloat16),
            pltpu.VMEM((slot_count, *tile), jnp.float32),
        ],
        "model",
    )

    def update(last):
        outs = [] if last else [shape(slot_count, jnp.bfloat16)]
        return call(
            update_kernel,
            [shape(tile_count, jnp.float32)] + outs,
            [SMEM, VMEM, VMEM, VMEM],
            [pltpu.VMEM((tile_count, *tile), jnp.float32)],
            "update",
        )

    def join(parts):
        count = parts[0].shape[0]
        whole = jax.ShapeDtypeStruct((count, wave_count, width), jnp.float32)
        return call(join_kernel, [whole], [SMEM] + [VMEM] * lo_count, [], "join")(ids, *parts)[0]

    def waves_of(array, d):
        cut = array.reshape(array.shape[0], lo_count, *tile)
        return lax.dynamic_index_in_dim(cut, lo ^ d, 1, keepdims=False)

    shared = [swap(model_blocks, d) for d in range(lo_count)]
    estimate, outgoing = pick(ids, sent_tiles, start_image)
    tiles = exchange(outgoing, "vox")
    models = stage(*shared)
    signals = jnp.concatenate([swap(waves_of(measured, d), d) for d in range(lo_count)])
    index = jnp.stack([block_slots, block_rows])
    index = jnp.stack(
        [swap(index, d) + jnp.array([[0], [d * row_count]], jnp.int32) for d in range(lo_count)]
    )
    gains = jnp.broadcast_to(
        lax.dynamic_slice_in_dim(step_size, lo * waves, waves)[:, None], tile
    )
    for iteration in range(ITERATIONS):
        total, residual = apply_model(index, signals, tiles, *models)
        total = total.reshape(vox_count * hi_count, capacity, *tile)
        parts = exchange(total, ("vox", "hi")).reshape(vox_count, hi_count, capacity, *tile)
        estimate, *outgoing = update(iteration == ITERATIONS - 1)(
            sent_tiles, gains, estimate, parts
        )
        if outgoing:
            tiles = exchange(*outgoing, "vox")
    residual = join(
        [swap(residual[d * row_count : (d + 1) * row_count], d) for d in range(lo_count)]
    )
    estimate = join([swap(estimate, d) for d in range(lo_count)])
    return (estimate, residual)


def solution(mesh):
    vox_count, chan_count = mesh.devices.shape
    lo_count = math.gcd(chan_count, 2)
    cut = Mesh(
        mesh.devices.reshape(vox_count, chan_count // lo_count, lo_count), ("vox", "hi", "lo")
    )
    everywhere = ("vox", "hi", "lo")
    in_specs = (
        P(everywhere, None, None),
        P("vox", None, None),
        P(everywhere, None, None),
        P(),
        P("vox", None, None),
        P(everywhere),
        P(everywhere),
    )
    out_specs = (P("vox", None, None), P(everywhere, None, None))
    return jax.shard_map(shards, mesh=cut, in_specs=in_specs, out_specs=out_specs, check_vma=False)
```

```python
import functools
import math

import jax
import jax.numpy as jnp
from jax import lax
from jax.experimental import pallas as pl
from jax.experimental.pallas import tpu as pltpu
from jax.sharding import Mesh, PartitionSpec as P

ITERATIONS = 4


VMEM = pl.BlockSpec(memory_space=pltpu.VMEM)
SMEM = pl.BlockSpec(memory_space=pltpu.SMEM)
PARAMS = pltpu.CompilerParams(vmem_limit_bytes=16 * 1024 * 1024)


def grouped(source, index, column, d, model, k, size, dims):
    left = [source[index[d, column, k + i]] for i in range(size)]
    blocks = [model[k + i] for i in range(size)]
    if size < 4:
        return [
            lax.dot_general(x, block, dims, preferred_element_type=jnp.float32)
            for x, block in zip(left, blocks)
        ]
    zero = jnp.zeros_like(left[0])
    rows = jnp.concatenate(
        [
            jnp.concatenate([x, zero] if i % 2 == 0 else [zero, x], axis=1)
            for i, x in enumerate(left)
        ],
        axis=0,
    )
    depth = dims[0][1][0]
    halves = [jnp.concatenate(blocks[n : n + 2], axis=depth) for n in (0, 2)]
    whole = jnp.concatenate(halves, axis=1 - depth)
    out = lax.dot_general(rows, whole, dims, preferred_element_type=jnp.float32)
    height, width = left[0].shape[0], out.shape[1] // 2
    return [
        out[i * height : (i + 1) * height, i // 2 * width : (i // 2 + 1) * width]
        for i in range(4)
    ]


def model_kernel(lo_count, index, measured, tiles, *refs):
    models = refs[:lo_count]
    out, residual, narrow, sums = refs[lo_count:]
    vox_count, hi_count, capacity = out.shape[:3]
    count = models[0].shape[0]
    residual[...] = measured[...]
    sums[...] = jnp.zeros_like(sums)
    for d, model in enumerate(models):
        for k in range(0, count, 4):
            for i, part in enumerate(
                grouped(
                    tiles, index, 0, d, model, k, min(4, count - k), (((1,), (1,)), ((), ()))
                )
            ):
                residual[index[d, 1, k + i]] -= part
    narrow[...] = residual[...].astype(jnp.bfloat16)
    for d, model in enumerate(models):
        for k in range(0, count, 4):
            for i, part in enumerate(
                grouped(
                    narrow, index, 1, d, model, k, min(4, count - k), (((1,), (0,)), ((), ()))
                )
            ):
                sums[index[d, 0, k + i]] += part
    for v in range(vox_count):
        piece = sums[v * capacity : (v + 1) * capacity].astype(jnp.bfloat16)
        for h in range(hi_count):
            out[v, h] = piece


def pick_tiles(table, image, out):
    _, vox_count, capacity = table.shape
    for v in range(vox_count):
        for s in range(capacity):
            tile = jnp.maximum(table[0, v, s], 0)
            out[v * capacity + s] = image[tile].astype(jnp.bfloat16)


def part_of(lo, size):
    return (slice(None), pl.ds(pl.multiple_of(lo * size, size), size))


def pick_kernel(lo, table, image, part, out):
    part[...] = image[part_of(lo[0], part.shape[1])]
    pick_tiles(table, part, out)


def update_kernel(table, gains, image, parts, estimate, *refs):
    *outs, gradient = refs
    vox_count, hi_count, capacity = parts.shape[:3]
    gradient[...] = jnp.zeros_like(gradient)
    for v in range(vox_count):
        for s in range(capacity):
            tile = jnp.maximum(table[0, v, s], 0)
            total = parts[v, 0, s].astype(jnp.float32)
            for h in range(1, hi_count):
                total = total + parts[v, h, s].astype(jnp.float32)
            gradient[tile] += total
    estimate[...] = jnp.maximum(image[...] + gains[...][None] * gradient[...], 0.0)
    if outs:
        pick_tiles(table, estimate, *outs)


def join_kernel(lo, *refs):
    *parts, out = refs
    for d, part in enumerate(parts):
        out[part_of(lo[0] ^ d, part.shape[1])] = part[...]


def shards(model_blocks, start_image, measured, step_size, sent_tiles, block_rows, block_slots):
    vox_count = lax.axis_size("vox")
    hi_count = lax.axis_size("hi")
    lo_count = lax.axis_size("lo")
    lo = lax.axis_index("lo")
    capacity = sent_tiles.shape[2]
    tile_count, wave_count, width = start_image.shape
    row_count = measured.shape[0]
    slot_count = vox_count * capacity
    waves = wave_count // lo_count
    tile = (waves, width)
    ids = lo.astype(jnp.int32)[None]

    def shape(count, dtype):
        return jax.ShapeDtypeStruct((count, *tile), dtype)

    def swap(array, d):
        pairs = [(i, i ^ d) for i in range(lo_count)]
        return lax.ppermute(array, "lo", pairs) if d else array

    def exchange(array, axes):
        return lax.all_to_all(array, axes, split_axis=0, concat_axis=0, tiled=True)

    def call(kernel, out_shape, in_specs, scratch, name):
        return pl.pallas_call(
            kernel,
            out_shape=out_shape,
            in_specs=in_specs,
            out_specs=[VMEM] * len(out_shape),
            scratch_shapes=scratch,
            compiler_params=PARAMS,
            name=name,
        )

    pick = call(
        pick_kernel,
        [shape(tile_count, jnp.float32), shape(slot_count, jnp.bfloat16)],
        [SMEM, SMEM, VMEM],
        [],
        "pick",
    )
    apply_model = call(
        functools.partial(model_kernel, lo_count),
        [
            jax.ShapeDtypeStruct((vox_count, hi_count, capacity, *tile), jnp.bfloat16),
            shape(lo_count * row_count, jnp.float32),
        ],
        [SMEM, VMEM, VMEM] + [VMEM] * lo_count,
        [
            pltpu.VMEM((lo_count * row_count, *tile), jnp.bfloat16),
            pltpu.VMEM((slot_count, *tile), jnp.float32),
        ],
        "model",
    )

    def update(last):
        outs = [] if last else [shape(slot_count, jnp.bfloat16)]
        return call(
            update_kernel,
            [shape(tile_count, jnp.float32)] + outs,
            [SMEM, VMEM, VMEM, VMEM],
            [pltpu.VMEM((tile_count, *tile), jnp.float32)],
            "update",
        )

    def join(parts):
        count = parts[0].shape[0]
        whole = jax.ShapeDtypeStruct((count, wave_count, width), jnp.float32)
        return call(join_kernel, [whole], [SMEM] + [VMEM] * lo_count, [], "join")(ids, *parts)[0]

    def waves_of(array, d):
        cut = array.reshape(array.shape[0], lo_count, *tile)
        return lax.dynamic_index_in_dim(cut, lo ^ d, 1, keepdims=False)

    models = [swap(model_blocks, d) for d in range(lo_count)]
    estimate, outgoing = pick(ids, sent_tiles, start_image)
    tiles = exchange(outgoing, "vox")
    signals = jnp.concatenate([swap(waves_of(measured, d), d) for d in range(lo_count)])
    index = jnp.stack([block_slots, block_rows])
    index = jnp.stack(
        [swap(index, d) + jnp.array([[0], [d * row_count]], jnp.int32) for d in range(lo_count)]
    )
    gains = jnp.broadcast_to(
        lax.dynamic_slice_in_dim(step_size, lo * waves, waves)[:, None], tile
    )
    for iteration in range(ITERATIONS):
        total, residual = apply_model(index, signals, tiles, *models)
        total = total.reshape(vox_count * hi_count, capacity, *tile)
        parts = exchange(total, ("vox", "hi")).reshape(vox_count, hi_count, capacity, *tile)
        estimate, *outgoing = update(iteration == ITERATIONS - 1)(
            sent_tiles, gains, estimate, parts
        )
        if outgoing:
            tiles = exchange(*outgoing, "vox")
    residual = join(
        [swap(residual[d * row_count : (d + 1) * row_count], d) for d in range(lo_count)]
    )
    estimate = join([swap(estimate, d) for d in range(lo_count)])
    return (estimate, residual)


def solution(mesh):
    vox_count, chan_count = mesh.devices.shape
    lo_count = math.gcd(chan_count, 2)
    cut = Mesh(
        mesh.devices.reshape(vox_count, chan_count // lo_count, lo_count), ("vox", "hi", "lo")
    )
    everywhere = ("vox", "hi", "lo")
    in_specs = (
        P(everywhere, None, None),
        P("vox", None, None),
        P(everywhere, None, None),
        P(),
        P("vox", None, None),
        P(everywhere),
        P(everywhere),
    )
    out_specs = (P("vox", None, None), P(everywhere, None, None))
    return jax.shard_map(shards, mesh=cut, in_specs=in_specs, out_specs=out_specs, check_vma=False)
```

```python
import functools
import math

import jax
import jax.numpy as jnp
from jax import lax
from jax.experimental import pallas as pl
from jax.experimental.pallas import tpu as pltpu
from jax.sharding import Mesh, PartitionSpec as P

ITERATIONS = 4


VMEM = pl.BlockSpec(memory_space=pltpu.VMEM)
SMEM = pl.BlockSpec(memory_space=pltpu.SMEM)
PARAMS = pltpu.CompilerParams(vmem_limit_bytes=16 * 1024 * 1024)


def grouped(source, index, column, d, model, k, size, dims):
    left = [source[index[d, column, k + i]] for i in range(size)]
    blocks = [model[k + i] for i in range(size)]
    if size < 4:
        return [
            lax.dot_general(x, block, dims, preferred_element_type=jnp.float32)
            for x, block in zip(left, blocks)
        ]
    zero = jnp.zeros_like(left[0])
    rows = jnp.concatenate(
        [
            jnp.concatenate([x, zero] if i % 2 == 0 else [zero, x], axis=1)
            for i, x in enumerate(left)
        ],
        axis=0,
    )
    depth = dims[0][1][0]
    halves = [jnp.concatenate(blocks[n : n + 2], axis=depth) for n in (0, 2)]
    whole = jnp.concatenate(halves, axis=1 - depth)
    out = lax.dot_general(rows, whole, dims, preferred_element_type=jnp.float32)
    height, width = left[0].shape[0], out.shape[1] // 2
    return [
        out[i * height : (i + 1) * height, i // 2 * width : (i // 2 + 1) * width]
        for i in range(4)
    ]


def model_kernel(lo_count, index, measured, tiles, *refs):
    models = refs[:lo_count]
    out, residual, narrow, sums = refs[lo_count:]
    vox_count, hi_count, capacity = out.shape[:3]
    count = models[0].shape[0]
    residual[...] = measured[...]
    sums[...] = jnp.zeros_like(sums)
    for d, model in enumerate(models):
        for k in range(0, count, 4):
            for i, part in enumerate(
                grouped(
                    tiles, index, 0, d, model, k, min(4, count - k), (((1,), (1,)), ((), ()))
                )
            ):
                residual[index[d, 1, k + i]] -= part
    narrow[...] = residual[...].astype(jnp.bfloat16)
    for d, model in enumerate(models):
        for k in range(0, count, 4):
            for i, part in enumerate(
                grouped(
                    narrow, index, 1, d, model, k, min(4, count - k), (((1,), (0,)), ((), ()))
                )
            ):
                sums[index[d, 0, k + i]] += part
    for v in range(vox_count):
        piece = sums[v * capacity : (v + 1) * capacity].astype(jnp.bfloat16)
        for h in range(hi_count):
            out[v, h] = piece


def pick_tiles(table, image, out):
    _, vox_count, capacity = table.shape
    for v in range(vox_count):
        for s in range(capacity):
            tile = jnp.maximum(table[0, v, s], 0)
            out[v * capacity + s] = image[tile].astype(jnp.bfloat16)


def part_of(lo, size):
    return (slice(None), pl.ds(pl.multiple_of(lo * size, size), size))


def pick_kernel(lo, table, image, part, out):
    part[...] = image[part_of(lo[0], part.shape[1])]
    pick_tiles(table, part, out)


def update_kernel(table, gains, image, parts, estimate, *refs):
    *outs, gradient = refs
    vox_count, hi_count, capacity = parts.shape[:3]
    gradient[...] = jnp.zeros_like(gradient)
    for v in range(vox_count):
        for s in range(capacity):
            tile = jnp.maximum(table[0, v, s], 0)
            total = parts[v, 0, s].astype(jnp.float32)
            for h in range(1, hi_count):
                total = total + parts[v, h, s].astype(jnp.float32)
            gradient[tile] += total
    estimate[...] = jnp.maximum(image[...] + gains[...][None] * gradient[...], 0.0)
    if outs:
        pick_tiles(table, estimate, *outs)


def join_kernel(lo, *refs):
    *parts, out = refs
    for d, part in enumerate(parts):
        out[part_of(lo[0] ^ d, part.shape[1])] = part[...]


def shards(model_blocks, start_image, measured, step_size, sent_tiles, block_rows, block_slots):
    vox_count = lax.axis_size("vox")
    hi_count = lax.axis_size("hi")
    lo_count = lax.axis_size("lo")
    lo = lax.axis_index("lo")
    capacity = sent_tiles.shape[2]
    tile_count, wave_count, width = start_image.shape
    row_count = measured.shape[0]
    slot_count = vox_count * capacity
    waves = wave_count // lo_count
    tile = (waves, width)
    ids = lo.astype(jnp.int32)[None]

    def shape(count, dtype):
        return jax.ShapeDtypeStruct((count, *tile), dtype)

    def swap(array, d):
        pairs = [(i, i ^ d) for i in range(lo_count)]
        return lax.ppermute(array, "lo", pairs) if d else array

    def exchange(array, axes):
        return lax.all_to_all(array, axes, split_axis=0, concat_axis=0, tiled=True)

    def call(kernel, out_shape, in_specs, scratch, name):
        return pl.pallas_call(
            kernel,
            out_shape=out_shape,
            in_specs=in_specs,
            out_specs=[VMEM] * len(out_shape),
            scratch_shapes=scratch,
            compiler_params=PARAMS,
            name=name,
        )

    pick = call(
        pick_kernel,
        [shape(tile_count, jnp.float32), shape(slot_count, jnp.bfloat16)],
        [SMEM, SMEM, VMEM],
        [],
        "pick",
    )
    apply_model = call(
        functools.partial(model_kernel, lo_count),
        [
            jax.ShapeDtypeStruct((vox_count, hi_count, capacity, *tile), jnp.bfloat16),
            shape(lo_count * row_count, jnp.float32),
        ],
        [SMEM, VMEM, VMEM] + [VMEM] * lo_count,
        [
            pltpu.VMEM((lo_count * row_count, *tile), jnp.bfloat16),
            pltpu.VMEM((slot_count, *tile), jnp.float32),
        ],
        "model",
    )

    def update(last):
        outs = [] if last else [shape(slot_count, jnp.bfloat16)]
        return call(
            update_kernel,
            [shape(tile_count, jnp.float32)] + outs,
            [SMEM, VMEM, VMEM, VMEM],
            [pltpu.VMEM((tile_count, *tile), jnp.float32)],
            "update",
        )

    def join(parts):
        count = parts[0].shape[0]
        whole = jax.ShapeDtypeStruct((count, wave_count, width), jnp.float32)
        return call(join_kernel, [whole], [SMEM] + [VMEM] * lo_count, [], "join")(ids, *parts)[0]

    def waves_of(array, d):
        cut = array.reshape(array.shape[0], lo_count, *tile)
        return lax.dynamic_index_in_dim(cut, lo ^ d, 1, keepdims=False)

    models = [swap(model_blocks, d) for d in range(lo_count)]
    estimate, outgoing = pick(ids, sent_tiles, start_image)
    tiles = exchange(outgoing, "vox")
    _, measured, block_slots, block_rows = lax.optimization_barrier(
        (outgoing, measured, block_slots, block_rows)
    )
    signals = jnp.concatenate([swap(waves_of(measured, d), d) for d in range(lo_count)])
    index = jnp.stack([block_slots, block_rows])
    index = jnp.stack(
        [swap(index, d) + jnp.array([[0], [d * row_count]], jnp.int32) for d in range(lo_count)]
    )
    gains = jnp.broadcast_to(
        lax.dynamic_slice_in_dim(step_size, lo * waves, waves)[:, None], tile
    )
    for iteration in range(ITERATIONS):
        total, residual = apply_model(index, signals, tiles, *models)
        total = total.reshape(vox_count * hi_count, capacity, *tile)
        parts = exchange(total, ("vox", "hi")).reshape(vox_count, hi_count, capacity, *tile)
        estimate, *outgoing = update(iteration == ITERATIONS - 1)(
            sent_tiles, gains, estimate, parts
        )
        if outgoing:
            tiles = exchange(*outgoing, "vox")
    residual = join(
        [swap(residual[d * row_count : (d + 1) * row_count], d) for d in range(lo_count)]
    )
    estimate = join([swap(estimate, d) for d in range(lo_count)])
    return (estimate, residual)


def solution(mesh):
    vox_count, chan_count = mesh.devices.shape
    lo_count = math.gcd(chan_count, 2)
    cut = Mesh(
        mesh.devices.reshape(vox_count, chan_count // lo_count, lo_count), ("vox", "hi", "lo")
    )
    everywhere = ("vox", "hi", "lo")
    in_specs = (
        P(everywhere, None, None),
        P("vox", None, None),
        P(everywhere, None, None),
        P(),
        P("vox", None, None),
        P(everywhere),
        P(everywhere),
    )
    out_specs = (P("vox", None, None), P(everywhere, None, None))
    return jax.shard_map(shards, mesh=cut, in_specs=in_specs, out_specs=out_specs, check_vma=False)
```
